32 devices in a mesh: ctx: 16 (over z, x, core), tp: 2 (over y).
Axes of the slice: x: 2, y: 2, z: 4, core: 2. Of those that a mesh axis runs over, the one named last changes fastest.
Arguments:
- queries: bfloat16 [4096, 4096], P('ctx', 'tp'), may hold values from -16 to 16
- unrotated_key_rows: bfloat16 [4096, 1024], P('ctx', 'tp'), may hold values from -16 to 16
- token_value_rows: bfloat16 [4096, 1024], P('ctx', 'tp'), may hold values from -6 to 6
- span_ids: int32 [32], P('ctx'), may hold values from 0 to 31, each once
- out_weight: bfloat16 [4096, 4096], P('tp', 'ctx'), may hold values from -0.25 to 0.25
Outputs:
- projected: bfloat16 [4096, 4096], P('ctx', 'tp')
The draws below stay inside these ranges and needn't reach their ends.
Inputs may be any that keep to these rules, and one draw needn't show every extreme that they name: `span_ids`: each span number appears once.
All inputs are finite; a program needn't handle non-finite values.
Results may differ from the reference program's by a relative error of at most 0.012.
The reference program's roundings to bfloat16 on the way count: a program that leaves them out, or rounds other values in their place, can miss the bound.
Values may be sent and summed in bfloat16 or wider, within the bound.
A program may use at most 128 MiB of HBM per device.

```python
import math
import jax
import jax.numpy as jnp
from jax import lax

D = 4096
QUERY_HEADS = 32
KEY_VALUE_HEADS = 8
HEAD_SIZE = 128
TOK_DEV = 256
SEQUENCE_TOKENS = 4096
SPANS = 32
N_TP = 2


def draw_queries(key, part):
    key = jax.random.fold_in(key, 11)
    array_dimensions = (SEQUENCE_TOKENS, QUERY_HEADS * HEAD_SIZE)
    return jnp.clip(1.5 * jax.random.normal(key, array_dimensions, jnp.float32), -9.0, 9.0).astype(jnp.bfloat16)


def draw_unrotated_key_rows(key, part):
    key = jax.random.fold_in(key, 12)
    array_dimensions = (SEQUENCE_TOKENS, KEY_VALUE_HEADS * HEAD_SIZE)
    return jnp.clip(1.5 * jax.random.normal(key, array_dimensions, jnp.float32), -9.0, 9.0).astype(jnp.bfloat16)


def block_scale(key, shape, shards, smallest, high):
    factor_of = 1.0
    for dim, blocks in shards:
        draws = jax.random.uniform(jax.random.fold_in(jax.random.fold_in(key, 6), dim), (blocks,), jnp.float32, smallest / len(shards), high / len(shards))
        factor_of = factor_of * jnp.repeat(jnp.exp(draws), shape[dim] // blocks).reshape((-1,) + (1,) * (len(shape) - 1 - dim))
    return factor_of


def bell_draw(rng, shape, scale, reach, shards=(), kind=jnp.bfloat16):
    array = scale * jax.random.normal(rng, shape, jnp.float32)
    if shards:
        array = array * block_scale(rng, shape, shards, -0.22, 0.18)
    return jnp.clip(array, -reach, reach).astype(kind)


def setup_inputs(seed: int = 0) -> dict:
    key_list = jax.random.split(jax.random.key(seed), 6)
    queries = draw_queries(jax.random.fold_in(key_list[5], 71), 0)
    unrotated_key_rows = draw_unrotated_key_rows(jax.random.fold_in(key_list[5], 71), 0)
    token_value_rows = bell_draw(key_list[2], (SEQUENCE_TOKENS, KEY_VALUE_HEADS * HEAD_SIZE), 1.0, 6.0, ((0, 16), (1, 2)))
    span_ids = jax.random.permutation(key_list[3], SPANS).astype(jnp.int32)
    out_weight = bell_draw(key_list[4], (QUERY_HEADS * HEAD_SIZE, D), (4 * HEAD_SIZE) ** -0.5, 0.25, ((0, 2), (1, 16)))
    return {"queries": queries, "unrotated_key_rows": unrotated_key_rows, "token_value_rows": token_value_rows, "span_ids": span_ids, "out_weight": out_weight}


ROPE_BASE = 500000.0
NEG_FILL = -1e+30

def positions(span_ids, span_len):
    total_rows = span_ids.shape[0] * span_len
    row_index = jnp.arange(total_rows, dtype=jnp.int32)
    return (span_ids[row_index // span_len] * span_len + row_index % span_len).astype(jnp.int32)

def apply_rotary(matrix, token_positions, head_dim):
    row_count = matrix.shape[0]
    split = head_dim // 2
    heads = matrix.astype(jnp.float32).reshape(row_count, -1, head_dim)
    freqs = ROPE_BASE ** (-(jnp.arange(split, dtype=jnp.float32) * (2.0 / head_dim)))
    angles = token_positions.astype(jnp.float32)[:, None] * freqs[None, :]
    cosine = jnp.cos(angles)[:, None, :]
    sine = jnp.sin(angles)[:, None, :]
    first_half = heads[..., :split]
    second_half = heads[..., split:]
    turned = jnp.concatenate([first_half * cosine - second_half * sine, first_half * sine + second_half * cosine], axis=-1)
    return turned.reshape(row_count, -1).astype(jnp.bfloat16)

def reference(queries, unrotated_key_rows, token_value_rows, span_ids, out_weight):
    total_row_count = queries.shape[0]
    heads_per_group = QUERY_HEADS // KEY_VALUE_HEADS
    token_positions = positions(span_ids, TOK_DEV // 2)
    rotated_query = apply_rotary(queries, token_positions, HEAD_SIZE).astype(jnp.float32).reshape(total_row_count, KEY_VALUE_HEADS, heads_per_group, HEAD_SIZE)
    key_head_rows = apply_rotary(unrotated_key_rows, token_positions, HEAD_SIZE).astype(jnp.float32).reshape(total_row_count, KEY_VALUE_HEADS, HEAD_SIZE).transpose(1, 0, 2)
    value_head_rows = token_value_rows.astype(jnp.float32).reshape(total_row_count, KEY_VALUE_HEADS, HEAD_SIZE).transpose(1, 0, 2)
    block_len = math.gcd(total_row_count, 512)
    factor = 1.0 / math.sqrt(HEAD_SIZE)

    def one_block(block_index):
        first_row = (block_index * block_len).astype(jnp.int32)
        q_block = lax.dynamic_slice_in_dim(rotated_query, first_row, block_len, 0)
        q_places = lax.dynamic_slice_in_dim(token_positions, first_row, block_len, 0)
        allowed = token_positions[None, :] <= q_places[:, None]

        def one_head(operands):
            q_head, k_head, v_head = operands
            scores = jnp.einsum('qgd,nd->gqn', q_head, k_head) * factor
            scores = jnp.where(allowed[None], scores, NEG_FILL)
            row_max = lax.optimization_barrier(jnp.max(scores, axis=-1, keepdims=True))
            weights = jnp.where(allowed[None], jnp.exp(scores - row_max), 0.0)
            denominator = lax.optimization_barrier(jnp.sum(weights, axis=-1))
            rounded = lax.optimization_barrier(weights.astype(jnp.bfloat16)).astype(jnp.float32)
            summed = jnp.einsum('gqn,nd->gqd', rounded, v_head)
            return (summed / denominator[..., None]).transpose(1, 0, 2)
        heads_out = lax.map(one_head, (q_block.transpose(1, 0, 2, 3), key_head_rows, value_head_rows))
        return heads_out.transpose(1, 0, 2, 3).reshape(block_len, QUERY_HEADS * HEAD_SIZE).astype(jnp.bfloat16)
    attended = lax.map(one_block, jnp.arange(total_row_count // block_len, dtype=jnp.int32)).reshape(total_row_count, QUERY_HEADS * HEAD_SIZE)
    per_group = QUERY_HEADS * HEAD_SIZE // N_TP

    def add_group(group_index, summed):
        first_col = (group_index * per_group).astype(jnp.int32)
        rows_part = lax.dynamic_slice_in_dim(attended, first_col, per_group, 1)
        weight_part = lax.dynamic_slice_in_dim(out_weight, first_col, per_group, 0)
        group_term = jnp.dot(rows_part, weight_part, preferred_element_type=jnp.float32)
        rounded = lax.optimization_barrier(group_term.astype(jnp.bfloat16)).astype(jnp.float32)
        return summed + rounded
    result = lax.fori_loop(jnp.int32(0), jnp.int32(N_TP), add_group, jnp.zeros((total_row_count, D), jnp.float32))
    return result.astype(jnp.bfloat16)
```

```python
import functools
import math

import jax
import jax.numpy as jnp
from jax import lax
from jax.experimental import pallas as pl
from jax.experimental.pallas import tpu as pltpu
from jax.sharding import PartitionSpec as P

HEAD_SIZE = 128


ROPE_BASE = 500000.0
NEG_FILL = -1e30


def positions(span_ids, span_len):
    total_rows = span_ids.shape[0] * span_len
    row_index = jnp.arange(total_rows, dtype=jnp.int32)
    return span_ids[row_index // span_len] * span_len + row_index % span_len


def apply_rotary(matrix, token_positions, head_dim):
    row_count = matrix.shape[0]
    split = head_dim // 2
    heads = matrix.astype(jnp.float32).reshape(row_count, -1, head_dim)
    freqs = ROPE_BASE ** (-(jnp.arange(split, dtype=jnp.float32) * (2.0 / head_dim)))
    angles = token_positions.astype(jnp.float32)[:, None] * freqs[None, :]
    cosine = jnp.cos(angles)[:, None, :]
    sine = jnp.sin(angles)[:, None, :]
    first_half = heads[..., :split]
    second_half = heads[..., split:]
    turned = jnp.concatenate(
        [first_half * cosine - second_half * sine, first_half * sine + second_half * cosine],
        axis=-1,
    )
    return turned.reshape(row_count, -1).astype(jnp.bfloat16)


def absorb(carry_in, q_tile, q_places, k_tile, v_tile, k_places):
    run_max, run_sum, run_acc = carry_in
    scores = jnp.einsum("qkgd,nkd->qkgn", q_tile, k_tile, preferred_element_type=jnp.float32) * (
        1.0 / math.sqrt(HEAD_SIZE)
    )
    allowed = (k_places[None, :] <= q_places[:, None])[:, None, None, :]
    scores = jnp.where(allowed, scores, NEG_FILL)
    new_max = jnp.maximum(run_max, jnp.max(scores, axis=-1))
    weights = jnp.where(allowed, jnp.exp(scores - new_max[..., None]), 0.0)
    fade = jnp.exp(run_max - new_max)
    new_sum = run_sum * fade + jnp.sum(weights, axis=-1)
    new_acc = run_acc * fade[..., None] + jnp.einsum(
        "qkgn,nkd->qkgd", weights.astype(jnp.bfloat16), v_tile, preferred_element_type=jnp.float32
    )
    return (new_max, new_sum, new_acc)


LANES = 128
EXP2_SCALE = math.log2(math.e) / math.sqrt(HEAD_SIZE)
MESH = pl.DeviceIdType.MESH
W_EARLY = 3


def fused_kernel(
    n,
    span_ref,
    freq_ref,
    q_ref,
    k_ref,
    v_ref,
    w_hbm,
    out_ref,
    kvb,
    wb,
    qs,
    m_s,
    l_s,
    acc_s,
    bias,
    places,
    att,
    term,
    peer,
    kv_send,
    kv_recv,
    kvx_send,
    kvx_recv,
    w_send,
    w_recv,
    wx_send,
    wx_recv,
    y_send,
    y_recv,
    local_sem,
):
    rows, out_cols = out_ref.shape
    span_len = rows // 2
    chips = n // 2
    half = chips // 2
    kv_heads = k_ref.shape[1] // HEAD_SIZE
    group = q_ref.shape[1] // k_ref.shape[1]
    w_rows = wb.shape[3]
    me = lax.axis_index("ctx")
    tp = lax.axis_index("tp")
    core = lax.rem(me, 2)
    chip = lax.div(me, 2)
    odd = lax.rem(chip, 2)
    pos = (1 - odd) * lax.div(chip, 2) + odd * (chips - 1 - lax.div(chip, 2))

    def chip_at(p):
        p = lax.rem(p + chips, chips)
        back = lax.div(p, half)
        return (1 - back) * (2 * p) + back * (2 * (chips - 1 - p) + 1)

    forward = chip_at(pos + 1) * 2 + core
    backward = chip_at(pos - 1) * 2 + core
    ring = (forward, backward)
    sibling = chip * 2 + (1 - core)
    other = 1 - tp

    barrier = pltpu.get_barrier_semaphore()
    for who in ((forward, tp), (backward, tp), (sibling, tp), (me, other)):
        pl.semaphore_signal(barrier, inc=1, device_id=who, device_id_type=MESH)

    def remote(src, dst, send, recv, who):
        return pltpu.make_async_remote_copy(
            src_ref=src, dst_ref=dst, send_sem=send, recv_sem=recv, device_id=who, device_id_type=MESH
        )

    def kv_ring(d, s):
        return remote(
            kvb.at[d, 0, s], kvb.at[d, 0, s + 1], kv_send.at[d, s], kv_recv.at[d, s + 1], (ring[d], tp)
        )

    def kv_share(d, s):
        return remote(
            kvb.at[d, 0, s], kvb.at[d, 1, s], kvx_send.at[d, s], kvx_recv.at[d, s], (sibling, tp)
        )

    def w_ring(d, j):
        return remote(
            wb.at[d, 0, j], wb.at[d, 0, j + 2], w_send.at[d, j], w_recv.at[d, j + 2], (ring[d], tp)
        )

    def w_share(d, j):
        return remote(
            wb.at[d, 0, j], wb.at[d, 1, j], wx_send.at[d, j], wx_recv.at[d, j], (sibling, tp)
        )

    def w_local(d, j):
        return pltpu.make_async_copy(
            w_hbm.at[pl.ds(j * w_rows, w_rows), pl.ds(d * LANES, LANES)], wb.at[d, 0, j], local_sem.at[d, j]
        )

    for d in range(2):
        for j in range(2):
            w_local(d, j).start()

    row = lax.broadcasted_iota(jnp.int32, (rows, LANES), 0)
    lane = lax.broadcasted_iota(jnp.int32, (rows, LANES), 1)
    first = row < span_len
    place = jnp.where(first, span_ref[0] * span_len + row, span_ref[1] * span_len + row - span_len)
    place = place.astype(jnp.float32)
    places[...] = place
    angles = place * freq_ref[...]
    cosine = jnp.cos(angles)
    sine = jnp.sin(angles)
    sine = jnp.where(lane < HEAD_SIZE // 2, -sine, sine)

    def rotate(x):
        x = x.astype(jnp.float32)
        return (x * cosine + pltpu.roll(x, HEAD_SIZE // 2, 1) * sine).astype(jnp.bfloat16)

    for h in range(kv_heads):
        cols = slice(h * HEAD_SIZE, (h + 1) * HEAD_SIZE)
        turned = rotate(k_ref[:, cols])
        for d in range(2):
            kvb[d, 0, 0, 0:span_len, cols] = turned[d * span_len : (d + 1) * span_len]
    for d in range(2):
        kvb[d, 0, 0, span_len : 2 * span_len, :] = v_ref[d * span_len : (d + 1) * span_len, :]
        kvb[d, 0, 0, 2 * span_len :, :] = jnp.full(
            (kvb.shape[3] - 2 * span_len, kvb.shape[4]), span_ref[d].astype(jnp.float32)
        ).astype(jnp.bfloat16)

    pl.semaphore_wait(barrier, 4)
    for d in range(2):
        kv_ring(d, 0).start()
        kv_share(d, 0).start()
    for j in range(2):
        for d in range(2):
            w_local(d, j).wait()
            w_ring(d, j).start()
            w_share(d, j).start()

    for h in range(kv_heads):
        for g in range(group):
            cols = slice((h * group + g) * HEAD_SIZE, (h * group + g + 1) * HEAD_SIZE)
            qs[h, g * rows : (g + 1) * rows, :] = rotate(q_ref[:, cols])
    m_s[...] = jnp.full(m_s.shape, NEG_FILL, jnp.float32)
    l_s[...] = jnp.zeros(l_s.shape, jnp.float32)
    acc_s[...] = jnp.zeros(acc_s.shape, jnp.float32)

    def w_step(j):
        for d in range(2):
            w_ring(d, j - 2).wait_recv()

            @pl.when(j < 2 * chips - 2)
            def _():
                w_ring(d, j).start()

            w_share(d, j).start()

    def attend(s):
        for d in range(2):
            kv_share(d, s).wait_recv()
        slots = [(d, c) for c in range(2) for d in range(2)]
        lanes_f = lax.broadcasted_iota(jnp.int32, (1, LANES), 1).astype(jnp.float32)
        for b, (d, c) in enumerate(slots):
            span = kvb[d, c, s, 2 * span_len :, 0:LANES].astype(jnp.float32)[0:1]
            key_place = span * span_len + lanes_f
            bias[:, b * LANES : (b + 1) * LANES] = jnp.where(key_place <= places[...], 0.0, NEG_FILL)

        def one_kv_head(h, carry):
            cols = pl.ds(pl.multiple_of(h * HEAD_SIZE, HEAD_SIZE), HEAD_SIZE)
            keys = jnp.concatenate([kvb[d, c, s, 0:span_len, cols] for d, c in slots], axis=0)
            values = jnp.concatenate([kvb[d, c, s, span_len : 2 * span_len, cols] for d, c in slots], axis=0)
            for g in range(group):
                part = slice(g * rows, (g + 1) * rows)
                scores = lax.dot_general(
                    qs[h, part, :], keys, (((1,), (1,)), ((), ())), preferred_element_type=jnp.float32
                )
                scores = scores + bias[...]
                tiles = [scores[:, b * LANES : (b + 1) * LANES] for b in range(4)]
                top = jnp.maximum(jnp.maximum(tiles[0], tiles[1]), jnp.maximum(tiles[2], tiles[3]))
                m_old = m_s[h, part, :]
                m_new = jnp.maximum(m_old, jnp.max(top, axis=1, keepdims=True))
                fade = jnp.exp2((m_old - m_new) * EXP2_SCALE)
                weights = [jnp.exp2((tile - m_new) * EXP2_SCALE) for tile in tiles]
                m_s[h, part, :] = m_new
                l_s[h, part, :] = l_s[h, part, :] * fade + (
                    (weights[0] + weights[1]) + (weights[2] + weights[3])
                )
                rounded = jnp.concatenate([w.astype(jnp.bfloat16) for w in weights], axis=1)
                acc_s[h, part, :] = acc_s[h, part, :] * fade + jnp.dot(
                    rounded, values, preferred_element_type=jnp.float32
                )
            return carry

        lax.fori_loop(0, kv_heads, one_kv_head, 0)

    def kv_step(s, carry):
        @pl.when(s < chips)
        def _():
            for d in range(2):
                kv_ring(d, s - 1).wait_recv()

                @pl.when(s < chips - 1)
                def _():
                    kv_ring(d, s).start()

                kv_share(d, s).start()

        @pl.when(jnp.logical_and(lax.rem(s, 2) == 0, lax.div(s, 2) + 1 < 2 * W_EARLY))
        def _():
            w_step(lax.div(s, 2) + 1)

        attend(s - 1)
        return carry

    lax.fori_loop(1, chips + 1, kv_step, 0)

    for h in range(kv_heads):
        for g in range(group):
            part = slice(g * rows, (g + 1) * rows)
            cols = slice((h * group + g) * HEAD_SIZE, (h * group + g + 1) * HEAD_SIZE)
            total = jnp.sum(l_s[h, part, :], axis=1, keepdims=True)
            att[:, cols] = (acc_s[h, part, :] / total).astype(jnp.bfloat16)

    def column(d, c, k):
        owner_chip = chip_at(pos - k if d == 0 else pos + k)
        owner = owner_chip * 2 + (core + c - 2 * c * core)
        return owner * (2 * LANES) + d * LANES

    def y_copy(d, c, k):
        return remote(
            term.at[d, c, k], peer.at[d, c, k], y_send.at[d, c, k], y_recv.at[d, c, k], (me, other)
        )

    def project(k):
        for j in range(2):
            for d in range(2):
                w_share(d, 2 * k + j).wait_recv()
        for c in range(2):
            for d in range(2):
                product = jnp.dot(
                    att[:, 0:w_rows], wb[d, c, 2 * k], preferred_element_type=jnp.float32
                ) + jnp.dot(
                    att[:, w_rows : 2 * w_rows], wb[d, c, 2 * k + 1], preferred_element_type=jnp.float32
                )
                term[d, c, k] = product.astype(jnp.bfloat16)

                @pl.when(lax.div(column(d, c, k), out_cols) != tp)
                def _():
                    y_copy(d, c, k).start()

    def finish(k):
        for c in range(2):
            for d in range(2):
                start = column(d, c, k)

                @pl.when(lax.div(start, out_cols) == tp)
                def _():
                    y_copy(d, c, k).wait_recv()
                    both = term[d, c, k].astype(jnp.float32) + peer[d, c, k].astype(jnp.float32)
                    cols = pl.ds(pl.multiple_of(lax.rem(start, out_cols), LANES), LANES)
                    out_ref[:, cols] = both.astype(jnp.bfloat16)

    def project_step(i, carry):
        @pl.when(jnp.logical_and(i >= W_EARLY, i < chips))
        def _():
            w_step(2 * i)
            w_step(2 * i + 1)

        @pl.when(i <= chips)
        def _():
            project(i - 1)

        @pl.when(i >= 2)
        def _():
            finish(i - 2)

        return carry

    lax.fori_loop(1, chips + 2, project_step, 0)

    def drain(s, carry):
        for d in range(2):

            @pl.when(s < chips - 1)
            def _():
                kv_ring(d, s).wait_send()
                w_ring(d, 2 * s).wait_send()
                w_ring(d, 2 * s + 1).wait_send()

            kv_share(d, s).wait_send()
            w_share(d, 2 * s).wait_send()
            w_share(d, 2 * s + 1).wait_send()
            for c in range(2):

                @pl.when(lax.div(column(d, c, s), out_cols) != tp)
                def _():
                    y_copy(d, c, s).wait_send()

        return carry

    lax.fori_loop(0, chips, drain, 0)


def fused(n, queries, unrotated_key_rows, token_value_rows, span_ids, out_weight):
    rows, q_cols = queries.shape
    kv_cols = unrotated_key_rows.shape[1]
    chips = n // 2
    kv_heads = kv_cols // HEAD_SIZE
    group_rows = rows * (q_cols // kv_cols)
    split = HEAD_SIZE // 2
    freqs = ROPE_BASE ** (-(jnp.arange(split, dtype=jnp.float32) * (2.0 / HEAD_SIZE)))
    freqs = jnp.concatenate([freqs, freqs]).reshape(1, HEAD_SIZE)
    vmem = pl.BlockSpec(memory_space=pltpu.VMEM)
    dma = pltpu.SemaphoreType.DMA
    state = pltpu.VMEM((kv_heads, group_rows, LANES), jnp.float32)
    terms = pltpu.VMEM((2, 2, chips, rows, LANES), jnp.bfloat16)
    return pl.pallas_call(
        functools.partial(fused_kernel, n),
        out_shape=jax.ShapeDtypeStruct((rows, n * out_weight.shape[1] // 2), jnp.bfloat16),
        in_specs=[
            pl.BlockSpec(memory_space=pltpu.SMEM),
            vmem,
            vmem,
            vmem,
            vmem,
            pl.BlockSpec(memory_space=pl.ANY),
        ],
        out_specs=vmem,
        scratch_shapes=[
            pltpu.VMEM((2, 2, chips, rows + 16, kv_cols), jnp.bfloat16),
            pltpu.VMEM((2, 2, 2 * chips, out_weight.shape[0] // 2, LANES), jnp.bfloat16),
            pltpu.VMEM((kv_heads, group_rows, HEAD_SIZE), jnp.bfloat16),
            state,
            state,
            state,
            pltpu.VMEM((rows, 4 * LANES), jnp.float32),
            pltpu.VMEM((rows, LANES), jnp.float32),
            pltpu.VMEM((rows, q_cols), jnp.bfloat16),
            terms,
            terms,
            dma((2, chips)),
            dma((2, chips)),
            dma((2, chips)),
            dma((2, chips)),
            dma((2, 2 * chips)),
            dma((2, 2 * chips)),
            dma((2, 2 * chips)),
            dma((2, 2 * chips)),
            dma((2, 2, chips)),
            dma((2, 2, chips)),
            dma((2, 2)),
        ],
        compiler_params=pltpu.CompilerParams(
            collective_id=0, has_side_effects=True, vmem_limit_bytes=60 * 2**20
        ),
        name="attention_projection",
    )(span_ids, freqs, queries, unrotated_key_rows, token_value_rows, out_weight)


def per_device(queries, unrotated_key_rows, token_value_rows, span_ids, out_weight):
    rows_here = queries.shape[0]
    span_len = rows_here // 2
    kv_here = unrotated_key_rows.shape[1] // HEAD_SIZE
    heads_per_group = queries.shape[1] // unrotated_key_rows.shape[1]
    token_positions = positions(span_ids, span_len)
    rotated_query = apply_rotary(queries, token_positions, HEAD_SIZE).reshape(
        rows_here, kv_here, heads_per_group, HEAD_SIZE
    )
    k_rot = apply_rotary(unrotated_key_rows, token_positions, HEAD_SIZE)
    start_state = (
        jnp.full((rows_here, kv_here, heads_per_group), NEG_FILL, jnp.float32),
        jnp.zeros((rows_here, kv_here, heads_per_group), jnp.float32),
        jnp.zeros((rows_here, kv_here, heads_per_group, HEAD_SIZE), jnp.float32),
    )
    key_piece = lax.all_gather(k_rot, "ctx", axis=0, tiled=True)
    value_piece = lax.all_gather(token_value_rows, "ctx", axis=0, tiled=True)
    place_piece = lax.all_gather(token_positions, "ctx", axis=0, tiled=True)
    block_len = math.gcd(key_piece.shape[0], 512)
    block_count = key_piece.shape[0] // block_len
    key_blocks = key_piece.reshape(block_count, block_len, kv_here, HEAD_SIZE)
    value_blocks = value_piece.reshape(block_count, block_len, kv_here, HEAD_SIZE)
    place_blocks = place_piece.reshape(block_count, block_len)

    def one_block(block_index, carry_now):
        key_block = lax.dynamic_index_in_dim(key_blocks, block_index, 0, keepdims=False)
        value_block = lax.dynamic_index_in_dim(value_blocks, block_index, 0, keepdims=False)
        place_block = lax.dynamic_index_in_dim(place_blocks, block_index, 0, keepdims=False)
        return absorb(
            carry_now, rotated_query, token_positions, key_block, value_block, place_block
        )

    run_max, run_sum, run_acc = lax.fori_loop(0, block_count, one_block, start_state)
    attended = (run_acc / run_sum[..., None]).astype(jnp.bfloat16).reshape(rows_here, -1)
    group_term = jnp.dot(
        attended,
        lax.all_gather(out_weight, "ctx", axis=1, tiled=True),
        preferred_element_type=jnp.float32,
    )
    return lax.psum_scatter(group_term.astype(jnp.bfloat16), "tp", scatter_dimension=1, tiled=True)


def solution(mesh):
    in_specs = (P("ctx", "tp"), P("ctx", "tp"), P("ctx", "tp"), P("ctx"), P("tp", "ctx"))
    out_specs = P("ctx", "tp")
    n = mesh.shape["ctx"]

    def body(queries, unrotated_key_rows, token_value_rows, span_ids, out_weight):
        args = (queries, unrotated_key_rows, token_value_rows, span_ids, out_weight)
        ring_fits = (
            mesh.shape["tp"] == 2
            and n % 4 == 0
            and n >= 8
            and queries.shape[0] == 2 * LANES
            and out_weight.shape[1] == 2 * LANES
        )
        return fused(n, *args) if ring_fits else per_device(*args)

    return jax.shard_map(body, mesh=mesh, in_specs=in_specs, out_specs=out_specs, check_vma=False)
```

```python
import functools
import math

import jax
import jax.numpy as jnp
from jax import lax
from jax.experimental import pallas as pl
from jax.experimental.pallas import tpu as pltpu
from jax.sharding import PartitionSpec as P

HEAD_SIZE = 128


ROPE_BASE = 500000.0
NEG_FILL = -1e30


def positions(span_ids, span_len):
    total_rows = span_ids.shape[0] * span_len
    row_index = jnp.arange(total_rows, dtype=jnp.int32)
    return span_ids[row_index // span_len] * span_len + row_index % span_len


def apply_rotary(matrix, token_positions, head_dim):
    row_count = matrix.shape[0]
    split = head_dim // 2
    heads = matrix.astype(jnp.float32).reshape(row_count, -1, head_dim)
    freqs = ROPE_BASE ** (-(jnp.arange(split, dtype=jnp.float32) * (2.0 / head_dim)))
    angles = token_positions.astype(jnp.float32)[:, None] * freqs[None, :]
    cosine = jnp.cos(angles)[:, None, :]
    sine = jnp.sin(angles)[:, None, :]
    first_half = heads[..., :split]
    second_half = heads[..., split:]
    turned = jnp.concatenate(
        [first_half * cosine - second_half * sine, first_half * sine + second_half * cosine],
        axis=-1,
    )
    return turned.reshape(row_count, -1).astype(jnp.bfloat16)


def absorb(carry_in, q_tile, q_places, k_tile, v_tile, k_places):
    run_max, run_sum, run_acc = carry_in
    scores = jnp.einsum("qkgd,nkd->qkgn", q_tile, k_tile, preferred_element_type=jnp.float32) * (
        1.0 / math.sqrt(HEAD_SIZE)
    )
    allowed = (k_places[None, :] <= q_places[:, None])[:, None, None, :]
    scores = jnp.where(allowed, scores, NEG_FILL)
    new_max = jnp.maximum(run_max, jnp.max(scores, axis=-1))
    weights = jnp.where(allowed, jnp.exp(scores - new_max[..., None]), 0.0)
    fade = jnp.exp(run_max - new_max)
    new_sum = run_sum * fade + jnp.sum(weights, axis=-1)
    new_acc = run_acc * fade[..., None] + jnp.einsum(
        "qkgn,nkd->qkgd", weights.astype(jnp.bfloat16), v_tile, preferred_element_type=jnp.float32
    )
    return (new_max, new_sum, new_acc)


LANES = 128
EXP2_SCALE = math.log2(math.e) / math.sqrt(HEAD_SIZE)
MESH = pl.DeviceIdType.MESH
W_PIECES = 4


def fused_kernel(
    n,
    span_ref,
    freq_ref,
    q_ref,
    k_ref,
    v_ref,
    w_hbm,
    out_ref,
    kvb,
    wb,
    qs,
    m_s,
    l_s,
    acc_s,
    bias,
    places,
    att,
    term,
    from_y,
    from_x,
    from_xy,
    kv_send,
    kv_recv,
    kvs_send,
    kvs_recv,
    kvx_send,
    kvx_recv,
    kvf_send,
    kvf_recv,
    w_send,
    w_recv,
    ws_send,
    ws_recv,
    att_send,
    att_recv,
    t_send,
    y_recv,
    x_recv,
    xy_recv,
    local_sem,
):
    rows, out_cols = out_ref.shape
    span_len = rows // 2
    depth = n // 4
    kv_heads = k_ref.shape[1] // HEAD_SIZE
    group = q_ref.shape[1] // k_ref.shape[1]
    w_rows, w_cols = wb.shape[3:]
    me = lax.axis_index("ctx")
    tp = lax.axis_index("tp")
    core = lax.rem(me, 2)
    side = lax.rem(lax.div(me, 2), 2)
    z = lax.div(me, 4)
    ahead = (me + 4, me - 4)
    has = (z < depth - 1, z > 0)
    sibling = me + 1 - 2 * core
    across = me + 2 - 4 * side
    other = 1 - tp

    def visit(i):
        z1, z0, i1, i0 = lax.div(z, 2), lax.rem(z, 2), lax.div(i, 2), lax.rem(i, 2)
        return (z1 + i1 - 2 * z1 * i1) * 2 + (z0 + i0 - 2 * z0 * i0)

    barrier = pltpu.get_barrier_semaphore()
    for who in ((sibling, tp), (across, tp), (me, other), (across, other)):
        pl.semaphore_signal(barrier, inc=1, device_id=who, device_id_type=MESH)
    for d in range(2):

        @pl.when(has[d])
        def _():
            pl.semaphore_signal(barrier, inc=1, device_id=(ahead[d], tp), device_id_type=MESH)

    def remote(src, dst, send, recv, who):
        return pltpu.make_async_remote_copy(
            src_ref=src, dst_ref=dst, send_sem=send, recv_sem=recv, device_id=who, device_id_type=MESH
        )

    def kv_move(d, b, p):
        slot = kvb.at[0, b, p]
        return remote(slot, slot, kv_send.at[d, b, p], kv_recv.at[b, p], (ahead[d], tp))

    def kv_share(b, p):
        return remote(
            kvb.at[0, b, p], kvb.at[1, b, p], kvs_send.at[b, p], kvs_recv.at[b, p], (sibling, tp)
        )

    def kv_cross(b, p):
        return remote(
            kvb.at[0, b, p], kvb.at[2, b, p], kvx_send.at[b, p], kvx_recv.at[b, p], (across, tp)
        )

    def kv_pass(b, p):
        return remote(
            kvb.at[2, b, p], kvb.at[3, b, p], kvf_send.at[b, p], kvf_recv.at[b, p], (sibling, tp)
        )

    def w_move(d, b, p):
        slot = wb.at[0, b, p]
        return remote(slot, slot, w_send.at[d, b, p], w_recv.at[b, p], (ahead[d], tp))

    def w_share(b, p):
        return remote(
            wb.at[0, b, p], wb.at[1, b, p], ws_send.at[b, p], ws_recv.at[b, p], (sibling, tp)
        )

    def w_local(p):
        return pltpu.make_async_copy(
            w_hbm.at[pl.ds(p * w_rows, w_rows), :], wb.at[0, z, p], local_sem.at[p]
        )

    def w_own(p):
        w_local(p).wait()
        for d in range(2):

            @pl.when(has[d])
            def _():
                w_move(d, z, p).start()

        w_share(z, p).start()

    for p in range(W_PIECES):
        w_local(p).start()

    row = lax.broadcasted_iota(jnp.int32, (rows, LANES), 0)
    lane = lax.broadcasted_iota(jnp.int32, (rows, LANES), 1)
    first = row < span_len
    place = jnp.where(first, span_ref[0] * span_len + row, span_ref[1] * span_len + row - span_len)
    place = place.astype(jnp.float32)
    places[...] = place
    angles = place * freq_ref[...]
    cosine = jnp.cos(angles)
    sine = jnp.sin(angles)
    sine = jnp.where(lane < HEAD_SIZE // 2, -sine, sine)

    def rotate(x):
        x = x.astype(jnp.float32)
        return (x * cosine + pltpu.roll(x, HEAD_SIZE // 2, 1) * sine).astype(jnp.bfloat16)

    for h in range(kv_heads):
        cols = slice(h * HEAD_SIZE, (h + 1) * HEAD_SIZE)
        turned = rotate(k_ref[:, cols])
        for d in range(2):
            kvb[0, z, d, 0:span_len, cols] = turned[d * span_len : (d + 1) * span_len]
    for d in range(2):
        kvb[0, z, d, span_len : 2 * span_len, :] = v_ref[d * span_len : (d + 1) * span_len, :]
        kvb[0, z, d, 2 * span_len :, :] = jnp.full(
            (kvb.shape[3] - 2 * span_len, kvb.shape[4]), span_ref[d].astype(jnp.float32)
        ).astype(jnp.bfloat16)

    pl.semaphore_wait(barrier, 4 + lax.div(z + depth - 1, depth) + lax.div(2 * depth - 2 - z, depth))
    for p in range(2):
        for d in range(2):

            @pl.when(has[d])
            def _():
                kv_move(d, z, p).start()

        kv_cross(z, p).start()
        kv_share(z, p).start()
    w_own(0)
    w_own(1)

    for h in range(kv_heads):
        for g in range(group):
            cols = slice((h * group + g) * HEAD_SIZE, (h * group + g + 1) * HEAD_SIZE)
            qs[h, g * rows : (g + 1) * rows, :] = rotate(q_ref[:, cols])
    m_s[...] = jnp.full(m_s.shape, NEG_FILL, jnp.float32)
    l_s[...] = jnp.zeros(l_s.shape, jnp.float32)
    acc_s[...] = jnp.zeros(acc_s.shape, jnp.float32)

    def arrivals(step, move, shares, pieces):
        for d in range(2):
            block = z - step if d == 0 else z + step

            @pl.when(block >= 0 if d == 0 else block < depth)
            def _():
                for p in pieces:
                    move(d, block, p).wait_recv()

                    @pl.when(has[d])
                    def _():
                        move(d, block, p).start()

                    for share in shares:
                        share(block, p).start()

    def attend(b, half):
        slots = [(2 * half + c, p) for c in range(2) for p in range(2)]
        lanes_f = lax.broadcasted_iota(jnp.int32, (1, LANES), 1).astype(jnp.float32)
        for t, (kind, p) in enumerate(slots):
            span = kvb[kind, b, p, 2 * span_len :, 0:LANES].astype(jnp.float32)[0:1]
            key_place = span * span_len + lanes_f
            bias[:, t * LANES : (t + 1) * LANES] = jnp.where(key_place <= places[...], 0.0, NEG_FILL)

        def one_kv_head(h, carry):
            cols = pl.ds(pl.multiple_of(h * HEAD_SIZE, HEAD_SIZE), HEAD_SIZE)
            keys = jnp.concatenate([kvb[kind, b, p, 0:span_len, cols] for kind, p in slots], axis=0)
            values = jnp.concatenate(
                [kvb[kind, b, p, span_len : 2 * span_len, cols] for kind, p in slots], axis=0
            )
            for g in range(group):
                part = slice(g * rows, (g + 1) * rows)
                scores = lax.dot_general(
                    qs[h, part, :], keys, (((1,), (1,)), ((), ())), preferred_element_type=jnp.float32
                )
                scores = scores + bias[...]
                tiles = [scores[:, t * LANES : (t + 1) * LANES] for t in range(4)]
                top = jnp.maximum(jnp.maximum(tiles[0], tiles[1]), jnp.maximum(tiles[2], tiles[3]))
                m_old = m_s[h, part, :]
                m_new = jnp.maximum(m_old, jnp.max(top, axis=1, keepdims=True))
                fade = jnp.exp2((m_old - m_new) * EXP2_SCALE)
                weights = [jnp.exp2((tile - m_new) * EXP2_SCALE) for tile in tiles]
                m_s[h, part, :] = m_new
                l_s[h, part, :] = l_s[h, part, :] * fade + (
                    (weights[0] + weights[1]) + (weights[2] + weights[3])
                )
                rounded = jnp.concatenate([w.astype(jnp.bfloat16) for w in weights], axis=1)
                acc_s[h, part, :] = acc_s[h, part, :] * fade + jnp.dot(
                    rounded, values, preferred_element_type=jnp.float32
                )
            return carry

        lax.fori_loop(0, kv_heads, one_kv_head, 0)

    def kv_step(i, carry):
        @pl.when(i < depth)
        def _():
            arrivals(i, kv_move, (kv_cross, kv_share), range(2))

        @pl.when(i == 1)
        def _():
            w_own(2)
            w_own(3)

        @pl.when(i == 2)
        def _():
            arrivals(1, w_move, (w_share,), (0, 1))

        @pl.when(i == 3)
        def _():
            arrivals(1, w_move, (w_share,), (2, 3))

        b = visit(i - 1)

        def one_half(half, carry):
            @pl.when(half == 0)
            def _():
                for p in range(2):
                    kv_share(b, p).wait_recv()

            @pl.when(half == 1)
            def _():
                for p in range(2):
                    kv_cross(b, p).wait_recv()
                    kv_pass(b, p).start()
                for p in range(2):
                    kv_pass(b, p).wait_recv()

            attend(b, half)
            return carry

        lax.fori_loop(0, 2, one_half, 0)
        return carry

    lax.fori_loop(1, depth + 1, kv_step, 0)

    def att_swap(h):
        width = group * HEAD_SIZE
        cols = pl.ds(h * width, width)
        return remote(
            att.at[0, :, cols], att.at[1, :, cols], att_send.at[h], att_recv.at[h], (across, tp)
        )

    for h in range(kv_heads):
        for g in range(group):
            part = slice(g * rows, (g + 1) * rows)
            cols = slice((h * group + g) * HEAD_SIZE, (h * group + g + 1) * HEAD_SIZE)
            total = jnp.sum(l_s[h, part, :], axis=1, keepdims=True)
            att[0, :, cols] = (acc_s[h, part, :] / total).astype(jnp.bfloat16)
        att_swap(h).start()

    def column(where, c, b):
        owner = b * 4 + where * 2 + (core + c - 2 * c * core)
        return owner * w_cols

    def home(b):
        return lax.div(b * 4 * w_cols, out_cols)

    def to_y(c, b):
        return remote(
            term.at[0, c, b], from_y.at[c, b], t_send.at[0, c, b], y_recv.at[c, b], (me, other)
        )

    def to_x(c, b):
        return remote(
            term.at[1, c, b], from_x.at[c, b], t_send.at[1, c, b], x_recv.at[c, b], (across, tp)
        )

    def to_xy(c, b):
        return remote(
            term.at[1, c, b], from_xy.at[c, b], t_send.at[1, c, b], xy_recv.at[c, b], (across, other)
        )

    def product(r, c, b):
        total = jnp.dot(att[r, :, 0:w_rows], wb[c, b, 0], preferred_element_type=jnp.float32)
        for p in range(1, W_PIECES):
            total += jnp.dot(
                att[r, :, p * w_rows : (p + 1) * w_rows], wb[c, b, p], preferred_element_type=jnp.float32
            )
        term[r, c, b] = total.astype(jnp.bfloat16)

    def project(b, r):
        for c in range(2):
            product(r, c, b)

            @pl.when(home(b) != tp)
            def _():
                (to_y if r == 0 else to_xy)(c, b).start()

            if r == 1:

                @pl.when(home(b) == tp)
                def _():
                    to_x(c, b).start()

    def finish(b):
        @pl.when(home(b) == tp)
        def _():
            for c in range(2):
                to_y(c, b).wait_recv()
                both = term[0, c, b].astype(jnp.float32) + from_y[c, b].astype(jnp.float32)
                cols = pl.ds(pl.multiple_of(lax.rem(column(side, c, b), out_cols), LANES), w_cols)
                out_ref[:, cols] = both.astype(jnp.bfloat16)
            for c in range(2):
                to_x(c, b).wait_recv()
                to_xy(c, b).wait_recv()
                both = from_x[c, b].astype(jnp.float32) + from_xy[c, b].astype(jnp.float32)
                cols = pl.ds(pl.multiple_of(lax.rem(column(1 - side, c, b), out_cols), LANES), w_cols)
                out_ref[:, cols] = both.astype(jnp.bfloat16)

    def w_ready(b):
        for p in range(W_PIECES):
            w_share(b, p).wait_recv()

    def project_step(i, carry):
        @pl.when(i >= 1)
        def _():
            @pl.when(i + 1 < depth)
            def _():
                arrivals(i + 1, w_move, (w_share,), range(W_PIECES))

            @pl.when(i == 1)
            def _():
                for h in range(kv_heads):
                    att_swap(h).wait_recv()
                project(visit(0), 1)

        @pl.when(i < depth)
        def _():
            b = visit(i)
            w_ready(b)
            project(b, 0)

            @pl.when(i >= 1)
            def _():
                project(b, 1)

        @pl.when(i >= 2)
        def _():
            finish(visit(i - 2))

        return carry

    lax.fori_loop(0, depth + 2, project_step, 0)

    for h in range(kv_heads):
        att_swap(h).wait_send()

    def drain(b, carry):
        gone = (jnp.logical_and(has[0], b <= z), jnp.logical_and(has[1], b >= z))
        for d in range(2):

            @pl.when(gone[d])
            def _():
                for p in range(2):
                    kv_move(d, b, p).wait_send()
                for p in range(W_PIECES):
                    w_move(d, b, p).wait_send()

        for p in range(2):
            kv_share(b, p).wait_send()
            kv_cross(b, p).wait_send()
            kv_pass(b, p).wait_send()
        for p in range(W_PIECES):
            w_share(b, p).wait_send()
        for c in range(2):
            to_x(c, b).wait_send()

            @pl.when(home(b) != tp)
            def _():
                to_y(c, b).wait_send()

        return carry

    lax.fori_loop(0, depth, drain, 0)


def fused(n, queries, unrotated_key_rows, token_value_rows, span_ids, out_weight):
    rows, q_cols = queries.shape
    kv_cols = unrotated_key_rows.shape[1]
    depth = n // 4
    kv_heads = kv_cols // HEAD_SIZE
    group_rows = rows * (q_cols // kv_cols)
    split = HEAD_SIZE // 2
    freqs = ROPE_BASE ** (-(jnp.arange(split, dtype=jnp.float32) * (2.0 / HEAD_SIZE)))
    freqs = jnp.concatenate([freqs, freqs]).reshape(1, HEAD_SIZE)
    vmem = pl.BlockSpec(memory_space=pltpu.VMEM)
    dma = pltpu.SemaphoreType.DMA
    state = pltpu.VMEM((kv_heads, group_rows, LANES), jnp.float32)
    w_cols = out_weight.shape[1]
    landed = pltpu.VMEM((2, depth, rows, w_cols), jnp.bfloat16)
    return pl.pallas_call(
        functools.partial(fused_kernel, n),
        out_shape=jax.ShapeDtypeStruct((rows, n * out_weight.shape[1] // 2), jnp.bfloat16),
        in_specs=[
            pl.BlockSpec(memory_space=pltpu.SMEM),
            vmem,
            vmem,
            vmem,
            vmem,
            pl.BlockSpec(memory_space=pl.ANY),
        ],
        out_specs=vmem,
        scratch_shapes=[
            pltpu.VMEM((4, depth, 2, rows + 16, kv_cols), jnp.bfloat16),
            pltpu.VMEM((2, depth, W_PIECES, out_weight.shape[0] // W_PIECES, w_cols), jnp.bfloat16),
            pltpu.VMEM((kv_heads, group_rows, HEAD_SIZE), jnp.bfloat16),
            state,
            state,
            state,
            pltpu.VMEM((rows, 4 * LANES), jnp.float32),
            pltpu.VMEM((rows, LANES), jnp.float32),
            pltpu.VMEM((2, rows, q_cols), jnp.bfloat16),
            pltpu.VMEM((2, 2, depth, rows, w_cols), jnp.bfloat16),
            landed,
            landed,
            landed,
            dma((2, depth, 2)),
            dma((depth, 2)),
            dma((depth, 2)),
            dma((depth, 2)),
            dma((depth, 2)),
            dma((depth, 2)),
            dma((depth, 2)),
            dma((depth, 2)),
            dma((2, depth, W_PIECES)),
            dma((depth, W_PIECES)),
            dma((depth, W_PIECES)),
            dma((depth, W_PIECES)),
            dma((kv_heads,)),
            dma((kv_heads,)),
            dma((2, 2, depth)),
            dma((2, depth)),
            dma((2, depth)),
            dma((2, depth)),
            dma((W_PIECES,)),
        ],
        compiler_params=pltpu.CompilerParams(
            collective_id=0, has_side_effects=True, vmem_limit_bytes=60 * 2**20
        ),
        name="attention_projection",
    )(span_ids, freqs, queries, unrotated_key_rows, token_value_rows, out_weight)


def per_device(queries, unrotated_key_rows, token_value_rows, span_ids, out_weight):
    rows_here = queries.shape[0]
    span_len = rows_here // 2
    kv_here = unrotated_key_rows.shape[1] // HEAD_SIZE
    heads_per_group = queries.shape[1] // unrotated_key_rows.shape[1]
    token_positions = positions(span_ids, span_len)
    rotated_query = apply_rotary(queries, token_positions, HEAD_SIZE).reshape(
        rows_here, kv_here, heads_per_group, HEAD_SIZE
    )
    k_rot = apply_rotary(unrotated_key_rows, token_positions, HEAD_SIZE)
    start_state = (
        jnp.full((rows_here, kv_here, heads_per_group), NEG_FILL, jnp.float32),
        jnp.zeros((rows_here, kv_here, heads_per_group), jnp.float32),
        jnp.zeros((rows_here, kv_here, heads_per_group, HEAD_SIZE), jnp.float32),
    )
    key_piece = lax.all_gather(k_rot, "ctx", axis=0, tiled=True)
    value_piece = lax.all_gather(token_value_rows, "ctx", axis=0, tiled=True)
    place_piece = lax.all_gather(token_positions, "ctx", axis=0, tiled=True)
    block_len = math.gcd(key_piece.shape[0], 512)
    block_count = key_piece.shape[0] // block_len
    key_blocks = key_piece.reshape(block_count, block_len, kv_here, HEAD_SIZE)
    value_blocks = value_piece.reshape(block_count, block_len, kv_here, HEAD_SIZE)
    place_blocks = place_piece.reshape(block_count, block_len)

    def one_block(block_index, carry_now):
        key_block = lax.dynamic_index_in_dim(key_blocks, block_index, 0, keepdims=False)
        value_block = lax.dynamic_index_in_dim(value_blocks, block_index, 0, keepdims=False)
        place_block = lax.dynamic_index_in_dim(place_blocks, block_index, 0, keepdims=False)
        return absorb(
            carry_now, rotated_query, token_positions, key_block, value_block, place_block
        )

    run_max, run_sum, run_acc = lax.fori_loop(0, block_count, one_block, start_state)
    attended = (run_acc / run_sum[..., None]).astype(jnp.bfloat16).reshape(rows_here, -1)
    group_term = jnp.dot(
        attended,
        lax.all_gather(out_weight, "ctx", axis=1, tiled=True),
        preferred_element_type=jnp.float32,
    )
    return lax.psum_scatter(group_term.astype(jnp.bfloat16), "tp", scatter_dimension=1, tiled=True)


def solution(mesh):
    in_specs = (P("ctx", "tp"), P("ctx", "tp"), P("ctx", "tp"), P("ctx"), P("tp", "ctx"))
    out_specs = P("ctx", "tp")
    n = mesh.shape["ctx"]

    def body(queries, unrotated_key_rows, token_value_rows, span_ids, out_weight):
        args = (queries, unrotated_key_rows, token_value_rows, span_ids, out_weight)
        ring_fits = (
            mesh.shape["tp"] == 2
            and n == 16
            and queries.shape[0] == 2 * LANES
            and out_weight.shape[1] == 2 * LANES
        )
        return fused(n, *args) if ring_fits else per_device(*args)

    return jax.shard_map(body, mesh=mesh, in_specs=in_specs, out_specs=out_specs, check_vma=False)
```

```python
import functools
import math

import jax
import jax.numpy as jnp
from jax import lax
from jax.experimental import pallas as pl
from jax.experimental.pallas import tpu as pltpu
from jax.sharding import PartitionSpec as P

HEAD_SIZE = 128


ROPE_BASE = 500000.0
NEG_FILL = -1e30


def positions(span_ids, span_len):
    total_rows = span_ids.shape[0] * span_len
    row_index = jnp.arange(total_rows, dtype=jnp.int32)
    return span_ids[row_index // span_len] * span_len + row_index % span_len


def apply_rotary(matrix, token_positions, head_dim):
    row_count = matrix.shape[0]
    split = head_dim // 2
    heads = matrix.astype(jnp.float32).reshape(row_count, -1, head_dim)
    freqs = ROPE_BASE ** (-(jnp.arange(split, dtype=jnp.float32) * (2.0 / head_dim)))
    angles = token_positions.astype(jnp.float32)[:, None] * freqs[None, :]
    cosine = jnp.cos(angles)[:, None, :]
    sine = jnp.sin(angles)[:, None, :]
    first_half = heads[..., :split]
    second_half = heads[..., split:]
    turned = jnp.concatenate(
        [first_half * cosine - second_half * sine, first_half * sine + second_half * cosine],
        axis=-1,
    )
    return turned.reshape(row_count, -1).astype(jnp.bfloat16)


def absorb(carry_in, q_tile, q_places, k_tile, v_tile, k_places):
    run_max, run_sum, run_acc = carry_in
    scores = jnp.einsum("qkgd,nkd->qkgn", q_tile, k_tile, preferred_element_type=jnp.float32) * (
        1.0 / math.sqrt(HEAD_SIZE)
    )
    allowed = (k_places[None, :] <= q_places[:, None])[:, None, None, :]
    scores = jnp.where(allowed, scores, NEG_FILL)
    new_max = jnp.maximum(run_max, jnp.max(scores, axis=-1))
    weights = jnp.where(allowed, jnp.exp(scores - new_max[..., None]), 0.0)
    fade = jnp.exp(run_max - new_max)
    new_sum = run_sum * fade + jnp.sum(weights, axis=-1)
    new_acc = run_acc * fade[..., None] + jnp.einsum(
        "qkgn,nkd->qkgd", weights.astype(jnp.bfloat16), v_tile, preferred_element_type=jnp.float32
    )
    return (new_max, new_sum, new_acc)


LANES = 128
EXP2_SCALE = math.log2(math.e) / math.sqrt(HEAD_SIZE)
MESH = pl.DeviceIdType.MESH
W_PIECES = 4


def fused_kernel(
    n,
    span_ref,
    freq_ref,
    q_ref,
    k_ref,
    v_ref,
    w_hbm,
    out_ref,
    kvb,
    wb,
    qs,
    m_s,
    l_s,
    acc_s,
    bias,
    places,
    att,
    term,
    from_y,
    from_x,
    from_xy,
    kv_send,
    kv_recv,
    kvs_send,
    kvs_recv,
    kvx_send,
    kvx_recv,
    kvf_send,
    kvf_recv,
    w_send,
    w_recv,
    ws_send,
    ws_recv,
    att_send,
    att_recv,
    t_send,
    y_recv,
    x_recv,
    xy_recv,
    local_sem,
):
    rows, out_cols = out_ref.shape
    span_len = rows // 2
    depth = n // 4
    kv_heads = k_ref.shape[1] // HEAD_SIZE
    group = q_ref.shape[1] // k_ref.shape[1]
    w_rows, w_cols = wb.shape[3:]
    me = lax.axis_index("ctx")
    tp = lax.axis_index("tp")
    core = lax.rem(me, 2)
    side = lax.rem(lax.div(me, 2), 2)
    z = lax.div(me, 4)
    ahead = (me + 4, me - 4)
    has = (z < depth - 1, z > 0)
    sibling = me + 1 - 2 * core
    across = me + 2 - 4 * side
    other = 1 - tp

    def visit(i):
        z1, z0, i1, i0 = lax.div(z, 2), lax.rem(z, 2), lax.div(i, 2), lax.rem(i, 2)
        return (z1 + i1 - 2 * z1 * i1) * 2 + (z0 + i0 - 2 * z0 * i0)

    barrier = pltpu.get_barrier_semaphore()
    for who in ((sibling, tp), (across, tp), (me, other), (across, other)):
        pl.semaphore_signal(barrier, inc=1, device_id=who, device_id_type=MESH)
    for d in range(2):

        @pl.when(has[d])
        def _():
            pl.semaphore_signal(barrier, inc=1, device_id=(ahead[d], tp), device_id_type=MESH)

    def remote(src, dst, send, recv, who):
        return pltpu.make_async_remote_copy(
            src_ref=src, dst_ref=dst, send_sem=send, recv_sem=recv, device_id=who, device_id_type=MESH
        )

    def kv_move(d, b, p):
        slot = kvb.at[0, b, p]
        return remote(slot, slot, kv_send.at[d, b, p], kv_recv.at[b, p], (ahead[d], tp))

    def kv_share(b, p):
        return remote(
            kvb.at[0, b, p], kvb.at[1, b, p], kvs_send.at[b, p], kvs_recv.at[b, p], (sibling, tp)
        )

    def kv_cross(b, p):
        return remote(
            kvb.at[0, b, p], kvb.at[2, b, p], kvx_send.at[b, p], kvx_recv.at[b, p], (across, tp)
        )

    def kv_pass(b, p):
        return remote(
            kvb.at[2, b, p], kvb.at[3, b, p], kvf_send.at[b, p], kvf_recv.at[b, p], (sibling, tp)
        )

    def w_move(d, b, p):
        slot = wb.at[0, b, p]
        return remote(slot, slot, w_send.at[d, b, p], w_recv.at[b, p], (ahead[d], tp))

    def w_share(b, p):
        return remote(
            wb.at[0, b, p], wb.at[1, b, p], ws_send.at[b, p], ws_recv.at[b, p], (sibling, tp)
        )

    def w_local(p):
        return pltpu.make_async_copy(
            w_hbm.at[pl.ds(p * w_rows, w_rows), :], wb.at[0, z, p], local_sem.at[p]
        )

    def w_own(p):
        w_local(p).wait()
        for d in range(2):

            @pl.when(has[d])
            def _():
                w_move(d, z, p).start()

        w_share(z, p).start()

    for p in range(W_PIECES):
        w_local(p).start()

    row = lax.broadcasted_iota(jnp.int32, (rows, LANES), 0)
    lane = lax.broadcasted_iota(jnp.int32, (rows, LANES), 1)
    first = row < span_len
    place = jnp.where(first, span_ref[0] * span_len + row, span_ref[1] * span_len + row - span_len)
    place = place.astype(jnp.float32)
    places[...] = place
    angles = place * freq_ref[...]
    cosine = jnp.cos(angles)
    sine = jnp.sin(angles)
    sine = jnp.where(lane < HEAD_SIZE // 2, -sine, sine)

    def rotate(x):
        x = x.astype(jnp.float32)
        return (x * cosine + pltpu.roll(x, HEAD_SIZE // 2, 1) * sine).astype(jnp.bfloat16)

    for h in range(kv_heads):
        cols = slice(h * HEAD_SIZE, (h + 1) * HEAD_SIZE)
        turned = rotate(k_ref[:, cols])
        for d in range(2):
            kvb[0, z, d, 0:span_len, cols] = turned[d * span_len : (d + 1) * span_len]
    for d in range(2):
        kvb[0, z, d, span_len : 2 * span_len, :] = v_ref[d * span_len : (d + 1) * span_len, :]
        kvb[0, z, d, 2 * span_len :, :] = jnp.full(
            (kvb.shape[3] - 2 * span_len, kvb.shape[4]), span_ref[d].astype(jnp.float32)
        ).astype(jnp.bfloat16)

    pl.semaphore_wait(barrier, 4 + lax.div(z + depth - 1, depth) + lax.div(2 * depth - 2 - z, depth))
    for p in range(2):
        for d in range(2):

            @pl.when(has[d])
            def _():
                kv_move(d, z, p).start()

        kv_cross(z, p).start()
        kv_share(z, p).start()
    w_own(0)

    for h in range(kv_heads):
        for g in range(group):
            cols = slice((h * group + g) * HEAD_SIZE, (h * group + g + 1) * HEAD_SIZE)
            qs[h, g * rows : (g + 1) * rows, :] = rotate(q_ref[:, cols])
    m_s[...] = jnp.full(m_s.shape, NEG_FILL, jnp.float32)
    l_s[...] = jnp.zeros(l_s.shape, jnp.float32)
    acc_s[...] = jnp.zeros(acc_s.shape, jnp.float32)

    def arrivals(step, move, shares, pieces):
        for p in pieces:
            for d in range(2):
                block = z - step if d == 0 else z + step

                @pl.when(block >= 0 if d == 0 else block < depth)
                def _():
                    move(d, block, p).wait_recv()

                    @pl.when(has[d])
                    def _():
                        move(d, block, p).start()

                    for share in shares:
                        share(block, p).start()

    def attend(b, half):
        slots = [(2 * half + c, p) for c in range(2) for p in range(2)]
        lanes_f = lax.broadcasted_iota(jnp.int32, (1, LANES), 1).astype(jnp.float32)
        for t, (kind, p) in enumerate(slots):
            span = kvb[kind, b, p, 2 * span_len :, 0:LANES].astype(jnp.float32)[0:1]
            key_place = span * span_len + lanes_f
            bias[:, t * LANES : (t + 1) * LANES] = jnp.where(key_place <= places[...], 0.0, NEG_FILL)

        def one_kv_head(h, carry):
            cols = pl.ds(pl.multiple_of(h * HEAD_SIZE, HEAD_SIZE), HEAD_SIZE)
            keys = jnp.concatenate([kvb[kind, b, p, 0:span_len, cols] for kind, p in slots], axis=0)
            values = jnp.concatenate(
                [kvb[kind, b, p, span_len : 2 * span_len, cols] for kind, p in slots], axis=0
            )
            for g in range(group):
                part = slice(g * rows, (g + 1) * rows)
                scores = lax.dot_general(
                    qs[h, part, :], keys, (((1,), (1,)), ((), ())), preferred_element_type=jnp.float32
                )
                scores = scores + bias[...]
                tiles = [scores[:, t * LANES : (t + 1) * LANES] for t in range(4)]
                top = jnp.maximum(jnp.maximum(tiles[0], tiles[1]), jnp.maximum(tiles[2], tiles[3]))
                m_old = m_s[h, part, :]
                m_new = jnp.maximum(m_old, jnp.max(top, axis=1, keepdims=True))
                fade = jnp.exp2((m_old - m_new) * EXP2_SCALE)
                weights = [jnp.exp2((tile - m_new) * EXP2_SCALE) for tile in tiles]
                m_s[h, part, :] = m_new
                l_s[h, part, :] = l_s[h, part, :] * fade + (
                    (weights[0] + weights[1]) + (weights[2] + weights[3])
                )
                rounded = jnp.concatenate([w.astype(jnp.bfloat16) for w in weights], axis=1)
                acc_s[h, part, :] = acc_s[h, part, :] * fade + jnp.dot(
                    rounded, values, preferred_element_type=jnp.float32
                )
            return carry

        lax.fori_loop(0, kv_heads, one_kv_head, 0)

    def kv_step(i, carry):
        @pl.when(i < depth)
        def _():
            arrivals(i, kv_move, (kv_cross, kv_share), range(2))

        @pl.when(i == 1)
        def _():
            w_own(1)

        @pl.when(i == 2)
        def _():
            w_own(2)
            w_own(3)

        @pl.when(i == 3)
        def _():
            arrivals(1, w_move, (w_share,), (0, 1))

        @pl.when(i == 4)
        def _():
            arrivals(1, w_move, (w_share,), (2, 3))

        b = visit(i - 1)

        def one_half(half, carry):
            @pl.when(half == 0)
            def _():
                for p in range(2):
                    kv_share(b, p).wait_recv()

            @pl.when(half == 1)
            def _():
                for p in range(2):
                    kv_cross(b, p).wait_recv()
                    kv_pass(b, p).start()
                for p in range(2):
                    kv_pass(b, p).wait_recv()

            attend(b, half)
            return carry

        lax.fori_loop(0, 2, one_half, 0)
        return carry

    lax.fori_loop(1, depth + 1, kv_step, 0)

    def att_swap(h):
        width = group * HEAD_SIZE
        cols = pl.ds(h * width, width)
        return remote(
            att.at[0, :, cols], att.at[1, :, cols], att_send.at[h], att_recv.at[h], (across, tp)
        )

    for h in range(kv_heads):
        for g in range(group):
            part = slice(g * rows, (g + 1) * rows)
            cols = slice((h * group + g) * HEAD_SIZE, (h * group + g + 1) * HEAD_SIZE)
            total = jnp.sum(l_s[h, part, :], axis=1, keepdims=True)
            att[0, :, cols] = (acc_s[h, part, :] / total).astype(jnp.bfloat16)
        att_swap(h).start()

    def column(where, c, b):
        owner = b * 4 + where * 2 + (core + c - 2 * c * core)
        return owner * w_cols

    def home(b):
        return lax.div(b * 4 * w_cols, out_cols)

    def to_y(c, b):
        return remote(
            term.at[0, c, b], from_y.at[c, b], t_send.at[0, c, b], y_recv.at[c, b], (me, other)
        )

    def to_x(c, b):
        return remote(
            term.at[1, c, b], from_x.at[c, b], t_send.at[1, c, b], x_recv.at[c, b], (across, tp)
        )

    def to_xy(c, b):
        return remote(
            term.at[1, c, b], from_xy.at[c, b], t_send.at[1, c, b], xy_recv.at[c, b], (across, other)
        )

    def product(r, c, b):
        total = jnp.dot(att[r, :, 0:w_rows], wb[c, b, 0], preferred_element_type=jnp.float32)
        for p in range(1, W_PIECES):
            total += jnp.dot(
                att[r, :, p * w_rows : (p + 1) * w_rows], wb[c, b, p], preferred_element_type=jnp.float32
            )
        term[r, c, b] = total.astype(jnp.bfloat16)

    def project(b, r):
        for c in range(2):
            product(r, c, b)

            @pl.when(home(b) != tp)
            def _():
                (to_y if r == 0 else to_xy)(c, b).start()

            if r == 1:

                @pl.when(home(b) == tp)
                def _():
                    to_x(c, b).start()

    def finish(b):
        @pl.when(home(b) == tp)
        def _():
            for c in range(2):
                to_y(c, b).wait_recv()
                both = term[0, c, b].astype(jnp.float32) + from_y[c, b].astype(jnp.float32)
                cols = pl.ds(pl.multiple_of(lax.rem(column(side, c, b), out_cols), LANES), w_cols)
                out_ref[:, cols] = both.astype(jnp.bfloat16)
            for c in range(2):
                to_x(c, b).wait_recv()
                to_xy(c, b).wait_recv()
                both = from_x[c, b].astype(jnp.float32) + from_xy[c, b].astype(jnp.float32)
                cols = pl.ds(pl.multiple_of(lax.rem(column(1 - side, c, b), out_cols), LANES), w_cols)
                out_ref[:, cols] = both.astype(jnp.bfloat16)

    def w_ready(b):
        for p in range(W_PIECES):
            w_share(b, p).wait_recv()

    def project_step(i, carry):
        @pl.when(i >= 1)
        def _():
            @pl.when(i == 1)
            def _():
                arrivals(2, w_move, (w_share,), range(W_PIECES))
                for h in range(kv_heads):
                    att_swap(h).wait_recv()
                project(visit(0), 1)

        @pl.when(i < depth)
        def _():
            b = visit(i)
            w_ready(b)
            project(b, 0)

            @pl.when(i >= 1)
            def _():
                project(b, 1)

            @pl.when(i == depth - 2)
            def _():
                arrivals(depth - 1, w_move, (w_share,), range(W_PIECES))

        @pl.when(i >= 2)
        def _():
            finish(visit(i - 2))

        return carry

    lax.fori_loop(0, depth + 2, project_step, 0)

    for h in range(kv_heads):
        att_swap(h).wait_send()

    def drain(b, carry):
        gone = (jnp.logical_and(has[0], b <= z), jnp.logical_and(has[1], b >= z))
        for d in range(2):

            @pl.when(gone[d])
            def _():
                for p in range(2):
                    kv_move(d, b, p).wait_send()
                for p in range(W_PIECES):
                    w_move(d, b, p).wait_send()

        for p in range(2):
            kv_share(b, p).wait_send()
            kv_cross(b, p).wait_send()
            kv_pass(b, p).wait_send()
        for p in range(W_PIECES):
            w_share(b, p).wait_send()
        for c in range(2):
            to_x(c, b).wait_send()

            @pl.when(home(b) != tp)
            def _():
                to_y(c, b).wait_send()

        return carry

    lax.fori_loop(0, depth, drain, 0)


def fused(n, queries, unrotated_key_rows, token_value_rows, span_ids, out_weight):
    rows, q_cols = queries.shape
    kv_cols = unrotated_key_rows.shape[1]
    depth = n // 4
    kv_heads = kv_cols // HEAD_SIZE
    group_rows = rows * (q_cols // kv_cols)
    split = HEAD_SIZE // 2
    freqs = ROPE_BASE ** (-(jnp.arange(split, dtype=jnp.float32) * (2.0 / HEAD_SIZE)))
    freqs = jnp.concatenate([freqs, freqs]).reshape(1, HEAD_SIZE)
    vmem = pl.BlockSpec(memory_space=pltpu.VMEM)
    dma = pltpu.SemaphoreType.DMA
    state = pltpu.VMEM((kv_heads, group_rows, LANES), jnp.float32)
    w_cols = out_weight.shape[1]
    landed = pltpu.VMEM((2, depth, rows, w_cols), jnp.bfloat16)
    return pl.pallas_call(
        functools.partial(fused_kernel, n),
        out_shape=jax.ShapeDtypeStruct((rows, n * out_weight.shape[1] // 2), jnp.bfloat16),
        in_specs=[
            pl.BlockSpec(memory_space=pltpu.SMEM),
            vmem,
            vmem,
            vmem,
            vmem,
            pl.BlockSpec(memory_space=pl.ANY),
        ],
        out_specs=vmem,
        scratch_shapes=[
            pltpu.VMEM((4, depth, 2, rows + 16, kv_cols), jnp.bfloat16),
            pltpu.VMEM((2, depth, W_PIECES, out_weight.shape[0] // W_PIECES, w_cols), jnp.bfloat16),
            pltpu.VMEM((kv_heads, group_rows, HEAD_SIZE), jnp.bfloat16),
            state,
            state,
            state,
            pltpu.VMEM((rows, 4 * LANES), jnp.float32),
            pltpu.VMEM((rows, LANES), jnp.float32),
            pltpu.VMEM((2, rows, q_cols), jnp.bfloat16),
            pltpu.VMEM((2, 2, depth, rows, w_cols), jnp.bfloat16),
            landed,
            landed,
            landed,
            dma((2, depth, 2)),
            dma((depth, 2)),
            dma((depth, 2)),
            dma((depth, 2)),
            dma((depth, 2)),
            dma((depth, 2)),
            dma((depth, 2)),
            dma((depth, 2)),
            dma((2, depth, W_PIECES)),
            dma((depth, W_PIECES)),
            dma((depth, W_PIECES)),
            dma((depth, W_PIECES)),
            dma((kv_heads,)),
            dma((kv_heads,)),
            dma((2, 2, depth)),
            dma((2, depth)),
            dma((2, depth)),
            dma((2, depth)),
            dma((W_PIECES,)),
        ],
        compiler_params=pltpu.CompilerParams(
            collective_id=0, has_side_effects=True, vmem_limit_bytes=60 * 2**20
        ),
        name="attention_projection",
    )(span_ids, freqs, queries, unrotated_key_rows, token_value_rows, out_weight)


def per_device(queries, unrotated_key_rows, token_value_rows, span_ids, out_weight):
    rows_here = queries.shape[0]
    span_len = rows_here // 2
    kv_here = unrotated_key_rows.shape[1] // HEAD_SIZE
    heads_per_group = queries.shape[1] // unrotated_key_rows.shape[1]
    token_positions = positions(span_ids, span_len)
    rotated_query = apply_rotary(queries, token_positions, HEAD_SIZE).reshape(
        rows_here, kv_here, heads_per_group, HEAD_SIZE
    )
    k_rot = apply_rotary(unrotated_key_rows, token_positions, HEAD_SIZE)
    start_state = (
        jnp.full((rows_here, kv_here, heads_per_group), NEG_FILL, jnp.float32),
        jnp.zeros((rows_here, kv_here, heads_per_group), jnp.float32),
        jnp.zeros((rows_here, kv_here, heads_per_group, HEAD_SIZE), jnp.float32),
    )
    key_piece = lax.all_gather(k_rot, "ctx", axis=0, tiled=True)
    value_piece = lax.all_gather(token_value_rows, "ctx", axis=0, tiled=True)
    place_piece = lax.all_gather(token_positions, "ctx", axis=0, tiled=True)
    block_len = math.gcd(key_piece.shape[0], 512)
    block_count = key_piece.shape[0] // block_len
    key_blocks = key_piece.reshape(block_count, block_len, kv_here, HEAD_SIZE)
    value_blocks = value_piece.reshape(block_count, block_len, kv_here, HEAD_SIZE)
    place_blocks = place_piece.reshape(block_count, block_len)

    def one_block(block_index, carry_now):
        key_block = lax.dynamic_index_in_dim(key_blocks, block_index, 0, keepdims=False)
        value_block = lax.dynamic_index_in_dim(value_blocks, block_index, 0, keepdims=False)
        place_block = lax.dynamic_index_in_dim(place_blocks, block_index, 0, keepdims=False)
        return absorb(
            carry_now, rotated_query, token_positions, key_block, value_block, place_block
        )

    run_max, run_sum, run_acc = lax.fori_loop(0, block_count, one_block, start_state)
    attended = (run_acc / run_sum[..., None]).astype(jnp.bfloat16).reshape(rows_here, -1)
    group_term = jnp.dot(
        attended,
        lax.all_gather(out_weight, "ctx", axis=1, tiled=True),
        preferred_element_type=jnp.float32,
    )
    return lax.psum_scatter(group_term.astype(jnp.bfloat16), "tp", scatter_dimension=1, tiled=True)


def solution(mesh):
    in_specs = (P("ctx", "tp"), P("ctx", "tp"), P("ctx", "tp"), P("ctx"), P("tp", "ctx"))
    out_specs = P("ctx", "tp")
    n = mesh.shape["ctx"]

    def body(queries, unrotated_key_rows, token_value_rows, span_ids, out_weight):
        args = (queries, unrotated_key_rows, token_value_rows, span_ids, out_weight)
        ring_fits = (
            mesh.shape["tp"] == 2
            and n == 16
            and queries.shape[0] == 2 * LANES
            and out_weight.shape[1] == 2 * LANES
        )
        return fused(n, *args) if ring_fits else per_device(*args)

    return jax.shard_map(body, mesh=mesh, in_specs=in_specs, out_specs=out_specs, check_vma=False)
```
